128 devices in a mesh: rep: 16 (over z, x_hi, core), tp: 8 (over x_lo, y).
Axes of the slice: x: 4 (x_hi: 2, x_lo: 2; x = x_hi * 2 + x_lo), y: 4, z: 4, core: 2. Of those that a mesh axis runs over, the one named last changes fastest.
Arguments:
- kv_master: float32 [16384, 2048], P(('rep', 'tp')), may hold values from -0.046875 to 0.046875
- hidden: bfloat16 [2, 64, 16384], P(None, 'rep', 'tp'), may hold values from -6 to 6
- queries: bfloat16 [2, 64, 16384], P(None, 'rep', 'tp'), may hold values from -34 to 34
- key_cache: bfloat16 [64, 8192, 1024], P('rep', None, 'tp'), may hold values from -6 to 6
- value_cache: bfloat16 [64, 8192, 1024], P('rep', None, 'tp'), may hold values from -6 to 6
- lengths: int32 [64], P('rep'), may hold values from 1 to 8192, as said below
Outputs:
- rollout_weight: bfloat16 [16384, 2048], P(None, 'tp')
- new_kv: bfloat16 [2, 64, 2048], P(None, 'rep', 'tp')
- attended: bfloat16 [2, 64, 16384], P(None, 'rep', 'tp')
The draws below stay inside these ranges and needn't reach their ends.
Inputs may be any that keep to these rules, and one draw needn't show every extreme that they name: `lengths`: some row holds exactly 8192 cached positions and some exactly 1.
All inputs are finite; a program needn't handle non-finite values.
Results may differ from the reference program's by a relative error of at most 0.0056.
Values may be sent and summed in bfloat16 or wider, within the bound.
No kernel may reach another device: no remote copies, remote signals or barrier semaphores. Data moves between devices by JAX's collectives and lax.ppermute only.
A program may use at most 128 MiB of HBM per device.

```python
import math
import jax
import jax.numpy as jnp
from jax import lax

D = 16384
KVH = 8
HD = 128
QH = 128
STEPS = 2
CTX = 8192
BATCH = 64


def draw_queries(key, part):
    key = jax.random.fold_in(key, 11)
    base_values = jnp.clip(jax.random.normal(key, (STEPS, BATCH, QH * HD), jnp.float32), -6.0, 6.0)
    return base_values.astype(jnp.bfloat16)


def draw_key_cache(key, part):
    key = jax.random.fold_in(key, 12)
    base_values = jnp.clip(jax.random.normal(key, (BATCH, CTX, KVH * HD), jnp.float32), -6.0, 6.0)
    return base_values.astype(jnp.bfloat16)


def draw_lengths(key, part):
    key = jax.random.fold_in(key, 13)
    level_key, value_key, pick_key = jax.random.split(key, 3)
    top_level = CTX.bit_length() - 1
    levels = jnp.minimum(jax.random.randint(level_key, (BATCH,), 0, 2 * top_level), top_level)
    lower_end = jnp.left_shift(jnp.int32(1), levels.astype(jnp.int32))
    drawn = jnp.minimum(jax.random.randint(value_key, (BATCH,), lower_end, 2 * lower_end), CTX)
    shuffled = jax.random.permutation(pick_key, BATCH)
    drawn = drawn.at[shuffled[0]].set(CTX).at[shuffled[1]].set(1)
    return drawn.astype(jnp.int32)


def level_of(own_key, extent, shards, least, high):
    gain = 1.0
    for position, shards_of in shards:
        steps = jax.random.uniform(jax.random.fold_in(jax.random.fold_in(own_key, 6), position), (shards_of,), jnp.float32, least / len(shards), high / len(shards))
        gain = gain * jnp.repeat(jnp.exp(steps), extent[position] // shards_of).reshape((-1,) + (1,) * (len(extent) - 1 - position))
    return gain


def bell_draw(stream_key, dims, scale, reach, shards=(), kind=jnp.bfloat16):
    factor_of = level_of(stream_key, dims, shards, -0.22, 0.18) if shards else 1.0
    entries = jax.random.normal(stream_key, dims, jnp.float32) * scale * factor_of
    return jnp.minimum(jnp.maximum(entries, -reach), reach).astype(kind)


def setup_inputs(seed: int = 0) -> dict:
    seeds = jax.random.split(jax.random.key(seed), 7)
    return {
        "kv_master": bell_draw(seeds[0], (D, KVH * 2 * HD), D ** -0.5, 0.046875, ((0, 128),), jnp.float32),
        "hidden": bell_draw(seeds[1], (STEPS, BATCH, D), 1.0, 6.0, ((1, 16), (2, 8))),
        "queries": draw_queries(jax.random.fold_in(seeds[6], 71), 0),
        "key_cache": draw_key_cache(jax.random.fold_in(seeds[6], 71), 0),
        "value_cache": bell_draw(seeds[4], (BATCH, CTX, KVH * HD), 1.0, 6.0, ((0, 16), (2, 8))),
        "lengths": draw_lengths(jax.random.fold_in(seeds[6], 71), 0),
    }


rope_base = 500000.0


def scaled_frequencies(width):
    pair_index = jnp.arange(width // 2, dtype=jnp.float32)
    base_freq = rope_base ** (-2.0 * pair_index / width)
    wavelength = 2.0 * math.pi / base_freq
    smooth = (8192.0 / wavelength - 1.0) / 3.0
    blended = (1.0 - smooth) * base_freq / 8.0 + smooth * base_freq
    return jnp.where(wavelength < 2048.0, base_freq, jnp.where(wavelength > 8192.0, base_freq / 8.0, blended))


def rotate_keys(key_part, positions):
    half_width = key_part.shape[-1] // 2
    inverse = scaled_frequencies(key_part.shape[-1])
    angles = positions.astype(jnp.float32)[..., None] * inverse
    cosine = jnp.cos(angles)
    sine_part = jnp.sin(angles)
    front_half = key_part[..., :half_width]
    back_half = key_part[..., half_width:]
    return jnp.concatenate([front_half * cosine - back_half * sine_part, back_half * cosine + front_half * sine_part], axis=-1)


def attend_row(query_heads, cache_keys, cache_values, length, fresh_pairs):
    step_count = query_heads.shape[0]
    cache_span = cache_keys.shape[0]
    score_scale = HD ** -0.5
    query_wide = query_heads.astype(jnp.float32)
    cache_scores = jnp.einsum("sgqd,pgd->sgqp", query_wide, cache_keys.astype(jnp.float32)) * score_scale
    visible = jnp.arange(cache_span, dtype=jnp.int32) < length
    cache_scores = jnp.where(visible[None, None, None, :], cache_scores, -jnp.inf)
    new_keys = fresh_pairs[:, :, 0, :].astype(jnp.float32)
    new_values = fresh_pairs[:, :, 1, :].astype(jnp.float32)
    new_scores = jnp.einsum("sgqd,jgd->sgqj", query_wide, new_keys) * score_scale
    causal = jnp.arange(step_count)[:, None] >= jnp.arange(step_count)[None, :]
    new_scores = jnp.where(causal[:, None, None, :], new_scores, -jnp.inf)
    row_max = jnp.maximum(jnp.max(cache_scores, axis=-1), jnp.max(new_scores, axis=-1))[..., None]
    cache_exp = jnp.exp(cache_scores - row_max)
    new_exp = jnp.exp(new_scores - row_max)
    denominator = jnp.sum(cache_exp, axis=-1, keepdims=True) + jnp.sum(new_exp, axis=-1, keepdims=True)
    cache_probs = (cache_exp / denominator).astype(jnp.bfloat16).astype(jnp.float32)
    new_probs = (new_exp / denominator).astype(jnp.bfloat16).astype(jnp.float32)
    mixed = jnp.einsum("sgqp,pgd->sgqd", cache_probs, cache_values.astype(jnp.float32))
    mixed = mixed + jnp.einsum("sgqj,jgd->sgqd", new_probs, new_values)
    return mixed.astype(jnp.bfloat16)


def reference(kv_master, hidden, queries, key_cache, value_cache, lengths):
    rollout_weight = kv_master.astype(jnp.bfloat16)
    step_count, batch_rows, feature_count = hidden.shape
    flat_hidden = hidden.reshape(step_count * batch_rows, feature_count)
    projected = jnp.dot(flat_hidden, rollout_weight, preferred_element_type=jnp.float32)
    paired = projected.reshape(step_count, batch_rows, KVH, 2, HD)
    positions = lengths[None, :] + jnp.arange(step_count, dtype=jnp.int32)[:, None]
    rotated = rotate_keys(paired[:, :, :, 0, :], positions[:, :, None])
    new_kv = jnp.stack([rotated, paired[:, :, :, 1, :]], axis=3).astype(jnp.bfloat16)
    groups = QH // KVH
    query_rows = jnp.moveaxis(queries.reshape(step_count, batch_rows, KVH, groups, HD), 1, 0)
    key_rows = key_cache.reshape(batch_rows, CTX, KVH, HD)
    value_rows = value_cache.reshape(batch_rows, CTX, KVH, HD)
    fresh_rows = jnp.moveaxis(new_kv, 1, 0)

    def one_row(items):
        return attend_row(items[0], items[1], items[2], items[3], items[4])

    outputs = lax.map(one_row, (query_rows, key_rows, value_rows, lengths, fresh_rows))
    attended = jnp.moveaxis(outputs, 0, 1).reshape(step_count, batch_rows, QH * HD)
    return rollout_weight, new_kv.reshape(step_count, batch_rows, KVH * 2 * HD), attended
```

```python
import math

import jax
import jax.numpy as jnp
from jax import lax
from jax.experimental import pallas as pl
from jax.experimental.pallas import tpu as pltpu
from jax.sharding import PartitionSpec as P

KVH = 8
HD = 128
QH = 128
GROUPS = QH // KVH
SCALE = HD ** (-0.5)

REP = 16
TP = 8
ROWS = 128
OWNED = TP * ROWS
HALF = OWNED // 2
COLS = 2 * HD
VMEM_BYTES = 60 * 2**20
CACHE_VMEM = 60 * 2**20
PLACE_VMEM = 60 * 2**20
PLACE_COST = pl.CostEstimate(flops=1000, bytes_accessed=1000, transcendentals=0)

rope_base = 500000.0

ANY = pl.BlockSpec(memory_space=pl.ANY)
SMEM = pl.BlockSpec(memory_space=pltpu.SMEM)
VMEM = pl.BlockSpec(memory_space=pltpu.VMEM)


def z_shift(step):
    return [(r, ((((r >> 2) + step) % 4) << 2) | (r & 3)) for r in range(REP)]


X_SWAP = [(r, r ^ 2) for r in range(REP)]
CORE_SWAP = [(r, r ^ 1) for r in range(REP)]


def send(value, pairs):
    return lax.ppermute(value, "rep", pairs)


def scaled_frequencies(width):
    pair_index = jnp.arange(width // 2, dtype=jnp.float32)
    base_freq = rope_base ** (-2.0 * pair_index / width)
    wavelength = 2.0 * math.pi / base_freq
    smooth = (8192.0 / wavelength - 1.0) / 3.0
    blended = (1.0 - smooth) * base_freq / 8.0 + smooth * base_freq
    return jnp.where(
        wavelength < 2048.0, base_freq, jnp.where(wavelength > 8192.0, base_freq / 8.0, blended)
    )


def rotation_tables(lengths, steps):
    positions = lengths[None, :] + jnp.arange(steps, dtype=jnp.int32)[:, None]
    angles = positions.reshape(-1, 1).astype(jnp.float32) * scaled_frequencies(HD)
    cosine, sine = jnp.cos(angles), jnp.sin(angles)
    return (
        jnp.concatenate([cosine, cosine], axis=-1),
        jnp.concatenate([-sine, sine], axis=-1),
    )


def pack_kernel(kv_ref, hid_ref, out_ref):
    steps, _, width = hid_ref.shape
    flat = jnp.concatenate([hid_ref[s].astype(jnp.float32) for s in range(steps)], axis=0)
    cut = [flat[:, c : c + COLS] for c in range(0, width, COLS)]
    cut = jnp.concatenate(cut, axis=0).astype(jnp.bfloat16)
    for t in range(TP):
        out_ref[t, :ROWS] = kv_ref[:, t * COLS : (t + 1) * COLS].astype(jnp.bfloat16)
        out_ref[t, ROWS:] = cut


def pack(kv_master, hidden):
    return pl.pallas_call(
        pack_kernel,
        in_specs=[VMEM, VMEM],
        out_specs=VMEM,
        out_shape=jax.ShapeDtypeStruct((TP, ROWS + hidden.size // COLS, COLS), jnp.bfloat16),
        compiler_params=pltpu.CompilerParams(vmem_limit_bytes=VMEM_BYTES),
    )(kv_master, hidden)


def cache_kernel(first, count, len_ref, q_ref, k_ref, v_ref, q_out, acc_out, m_out, l_out, q_scr, s_scr):
    i = pl.program_id(0)
    steps, rows = q_ref.shape[0], q_ref.shape[1]
    span = k_ref.shape[1]
    chunk = 2048

    @pl.when(i == 0)
    def _():
        flat = jnp.concatenate([q_ref[s].astype(jnp.float32) for s in range(steps)], axis=0)
        for g in range(GROUPS):
            q_scr[pl.ds(g, steps * rows, stride=GROUPS), :] = flat[:, g * HD : (g + 1) * HD]
        q_out[...] = q_scr[...].reshape(q_out.shape).astype(q_out.dtype)

    b = first + i
    base = [pl.multiple_of((s * rows + b) * GROUPS, GROUPS) for s in range(steps)]
    q = jnp.concatenate([q_scr[pl.ds(o, GROUPS), :] for o in base], axis=0).astype(jnp.bfloat16)
    length = len_ref[b]
    top = jnp.full((steps * GROUPS, 1), -jnp.inf, jnp.float32)
    for c in range(span // chunk):
        keys = k_ref[0, c * chunk : (c + 1) * chunk, :]
        scores = (
            lax.dot_general(q, keys, (((1,), (1,)), ((), ())), preferred_element_type=jnp.float32)
            * SCALE
        )
        place = c * chunk + lax.broadcasted_iota(jnp.int32, scores.shape, 1)
        scores = jnp.where(place < length, scores, -jnp.inf)
        s_scr[:, c * chunk : (c + 1) * chunk] = scores
        top = jnp.maximum(top, jnp.max(scores, axis=-1, keepdims=True))
    total = jnp.zeros((steps * GROUPS, 1), jnp.float32)
    acc = jnp.zeros((steps * GROUPS, HD), jnp.float32)
    for c in range(span // chunk):
        weights = jnp.exp(s_scr[:, c * chunk : (c + 1) * chunk] - top)
        total = total + jnp.sum(weights, axis=-1, keepdims=True)
        acc = acc + jnp.dot(
            weights.astype(jnp.bfloat16),
            v_ref[0, c * chunk : (c + 1) * chunk, :],
            preferred_element_type=jnp.float32,
        )
    for s in range(steps):
        part = slice(s * GROUPS, (s + 1) * GROUPS)
        place = s * count + i
        acc_out[place] = acc[part]
        m_out[place] = jnp.broadcast_to(top[part], (GROUPS, HD))
        l_out[place] = jnp.broadcast_to(total[part], (GROUPS, HD))


def attend_cache(queries, key_cache, value_cache, lengths, first, count):
    steps, rows, width = queries.shape
    span = key_cache.shape[1]
    part = jax.ShapeDtypeStruct((steps * count, GROUPS, HD), jnp.float32)
    return pl.pallas_call(
        lambda *refs: cache_kernel(first, count, *refs),
        grid=(count,),
        in_specs=[
            SMEM,
            pl.BlockSpec((steps, rows, width), lambda i: (0, 0, 0)),
            pl.BlockSpec((1, span, HD), lambda i: (first + i, 0, 0)),
            pl.BlockSpec((1, span, HD), lambda i: (first + i, 0, 0)),
        ],
        out_specs=[pl.BlockSpec((steps * rows, GROUPS, HD), lambda i: (0, 0, 0))]
        + [pl.BlockSpec(part.shape, lambda i: (0, 0, 0))] * 3,
        out_shape=[jax.ShapeDtypeStruct((steps * rows, GROUPS, HD), jnp.bfloat16)] + [part] * 3,
        scratch_shapes=[
            pltpu.VMEM((steps * rows * GROUPS, HD), jnp.float32),
            pltpu.VMEM((steps * GROUPS, span), jnp.float32),
        ],
        compiler_params=pltpu.CompilerParams(vmem_limit_bytes=CACHE_VMEM),
        cost_estimate=pl.CostEstimate(
            flops=4 * count * steps * GROUPS * span * HD,
            bytes_accessed=4 * count * span * HD,
            transcendentals=count * steps * GROUPS * span,
        ),
    )(lengths, queries, key_cache, value_cache)


def place_pieces(spots, where_ref, hid_ref, piece_refs, out_ref, buf, in_sem, out_sem):
    rep = where_ref[0]
    copies, offset = [], 0
    for i, (_, _, _, _, count) in enumerate(spots):
        copy = pltpu.make_async_copy(piece_refs[i], buf.at[pl.ds(offset, count)], in_sem.at[i])
        copy.start()
        copies.append((copy, offset))
        offset += count
    line = hid_ref.shape[1] // (2 * OWNED // COLS)
    total = jnp.zeros((line, COLS), jnp.float32)
    writes = []
    for i, (dz, dx, dc, first, count) in enumerate(spots):
        copy, offset = copies[i]
        copy.wait()
        owner = ((((rep >> 2) + dz) & 3) << 2) | ((rep & 3) ^ (2 * dx + dc))
        start = pl.multiple_of(owner * OWNED + first, ROWS)
        write = pltpu.make_async_copy(
            buf.at[pl.ds(offset, count)], out_ref.at[pl.ds(start, count)], out_sem.at[i]
        )
        write.start()
        writes.append(write)
        rows = pl.ds(pl.multiple_of((owner & 1) * (OWNED // COLS * line), 16), OWNED // COLS * line)
        blocks = hid_ref[owner >> 1, rows, :].astype(jnp.float32)
        for c in range(0, count, COLS):
            part = (first + c) // COLS * line
            total = total + jnp.dot(
                blocks[part : part + line].astype(jnp.bfloat16),
                buf[offset + c : offset + c + COLS, :],
                preferred_element_type=jnp.float32,
            )
    return total, writes


def early_kernel(spots, follows, where_ref, hid_ref, *refs):
    if follows:
        before_ref, _, *refs = refs
    count = len(spots)
    out_ref, sum_ref, buf, in_sem, out_sem = refs[count:]
    total, writes = place_pieces(
        spots, where_ref, hid_ref, refs[:count], out_ref, buf, in_sem, out_sem
    )
    sum_ref[...] = total + before_ref[...] if follows else total
    for write in writes:
        write.wait()


def late_kernel(spots, steps, rows, groups, where_ref, hid_ref, sum_ref, cos_ref, sin_ref, *refs):
    cached = [refs[4 * i : 4 * i + 4] for i in range(len(groups))]
    refs = refs[4 * len(groups) + 1 :]
    count = len(spots)
    out_ref, kv_ref, att_ref, buf, turn, in_sem, out_sem = refs[count:]
    total, writes = place_pieces(
        spots, where_ref, hid_ref, refs[:count], out_ref, buf, in_sem, out_sem
    )
    heads = steps * rows * GROUPS

    def join(which):
        return jnp.concatenate(
            [
                group[which][s * n : (s + 1) * n].reshape(n * GROUPS, HD)
                for s in range(steps)
                for group, n in zip(cached, groups)
            ],
            axis=0,
        )

    acc, old_top, old_total = join(1), join(2)[:, :1], join(3)[:, :1]
    total = total + sum_ref[...]
    keys = total[:, :HD]
    keys = keys * cos_ref[...] + pltpu.roll(keys, HD // 2, 1) * sin_ref[...]
    keys = keys.astype(jnp.bfloat16)
    values = total[:, HD:].astype(jnp.bfloat16)
    for s in range(steps):
        kv_ref[s, :, :HD] = keys[s * rows : (s + 1) * rows]
        kv_ref[s, :, HD:] = values[s * rows : (s + 1) * rows]
    scores = (
        lax.dot_general(
            cached[0][0][...].reshape(heads, HD),
            keys,
            (((1,), (1,)), ((), ())),
            preferred_element_type=jnp.float32,
        )
        * SCALE
    )
    line = lax.broadcasted_iota(jnp.int32, scores.shape, 0) // GROUPS
    column = lax.broadcasted_iota(jnp.int32, scores.shape, 1)
    seen = (line % rows == column % rows) & (column // rows <= line // rows)
    scores = jnp.where(seen, scores, -jnp.inf)
    top = jnp.maximum(old_top, jnp.max(scores, axis=-1, keepdims=True))
    fresh = jnp.exp(scores - top)
    fade = jnp.exp(old_top - top)
    denominator = old_total * fade + jnp.sum(fresh, axis=-1, keepdims=True)
    mixed = acc * (fade / denominator) + jnp.dot(
        (fresh / denominator).astype(jnp.bfloat16), values, preferred_element_type=jnp.float32
    )
    turn[...] = mixed
    for g in range(GROUPS):
        head = turn[pl.ds(g, steps * rows, stride=GROUPS), :].astype(jnp.bfloat16)
        for s in range(steps):
            att_ref[s, :, g * HD : (g + 1) * HD] = head[s * rows : (s + 1) * rows]
    for write in writes:
        write.wait()


def scratch(spots):
    return (
        pltpu.VMEM((sum(s[4] for s in spots), COLS), jnp.bfloat16),
        [pltpu.SemaphoreType.DMA((len(spots),)), pltpu.SemaphoreType.DMA((len(spots),))],
    )


def place_early(where, hid, before, pieces):
    spots = [p[1:] for p in pieces]
    buf, sems = scratch(spots)
    return pl.pallas_call(
        lambda *refs: early_kernel(spots, bool(before), *refs),
        in_specs=[SMEM, VMEM] + [VMEM, ANY][: len(before)] + [ANY] * len(pieces),
        out_specs=[VMEM, ANY][::-1],
        out_shape=[
            jax.ShapeDtypeStruct((REP * OWNED, COLS), jnp.bfloat16),
            jax.ShapeDtypeStruct((hid.shape[1] * COLS // (2 * OWNED), COLS), jnp.float32),
        ],
        scratch_shapes=[buf, *sems],
        input_output_aliases={3: 0} if before else {},
        compiler_params=pltpu.CompilerParams(vmem_limit_bytes=PLACE_VMEM),
        cost_estimate=PLACE_COST,
    )(where, hid, *before, *[p[0] for p in pieces])


def place_late(where, hid, partial, cosine, sine, cached, placed, pieces, steps, rows, groups):
    spots = [p[1:] for p in pieces]
    buf, sems = scratch(spots)
    small = 4 + 4 * len(groups)
    return pl.pallas_call(
        lambda *refs: late_kernel(spots, steps, rows, groups, *refs),
        in_specs=[SMEM] + [VMEM] * small + [ANY] * (1 + len(pieces)),
        out_specs=[ANY, VMEM, VMEM],
        out_shape=[
            jax.ShapeDtypeStruct((REP * OWNED, COLS), jnp.bfloat16),
            jax.ShapeDtypeStruct((steps, rows, COLS), jnp.bfloat16),
            jax.ShapeDtypeStruct((steps, rows, GROUPS * HD), jnp.bfloat16),
        ],
        scratch_shapes=[buf, pltpu.VMEM((steps * rows * GROUPS, HD), jnp.float32), *sems],
        input_output_aliases={1 + small: 0},
        compiler_params=pltpu.CompilerParams(vmem_limit_bytes=PLACE_VMEM),
        cost_estimate=PLACE_COST,
    )(where, hid, partial, cosine, sine, *cached, placed, *[p[0] for p in pieces])


def after(value, *others):
    return lax.optimization_barrier((value, *others))[0]


def local(kv_master, hidden, queries, key_cache, value_cache, lengths):
    steps, rows, _ = hidden.shape
    where = lax.axis_index("rep").astype(jnp.int32).reshape(1)

    moved = lax.all_to_all(pack(kv_master, hidden), "tp", split_axis=0, concat_axis=0, tiled=True)
    owned, hid = moved[:, :ROWS], moved[:, ROWS:]
    low, high = owned[: TP // 2].reshape(HALF, COLS), owned[TP // 2 :].reshape(HALF, COLS)
    cosine, sine = rotation_tables(lengths, steps)
    cached = attend_cache(queries, key_cache, value_cache, lengths, 0, rows)
    owned, low, high, *cached = lax.optimization_barrier((owned, low, high, *cached))
    owned = owned.reshape(OWNED, COLS)

    up, down = z_shift(1), z_shift(-1)
    near_x = send(owned, X_SWAP)
    low_b, high_a = send(low, up), send(high, down)
    low_a, high_b = send(low, down), send(high, up)
    low_b, high_a, cosine, sine = lax.optimization_barrier((low_b, high_a, cosine, sine))
    far_low, far_high = send(low_b, up), send(high_a, down)
    below_x, above_x = send(near_x, up), send(near_x, down)
    far_low_x, far_high_x = send(far_low, X_SWAP), send(far_high, X_SWAP)

    def both(pieces, *first):
        values = lax.optimization_barrier(tuple(p[0] for p in pieces) + first)
        pieces = [(v, *p[1:]) for v, p in zip(values, pieces)]
        return pieces + [(send(p[0], CORE_SWAP), p[1], p[2], 1, p[4], p[5]) for p in pieces]

    pieces = [
        (owned, 0, 0, 0, 0, OWNED),
        (near_x, 0, 1, 0, 0, OWNED),
        (low_b, 3, 0, 0, 0, HALF),
        (low_a, 1, 0, 0, 0, HALF),
        (high_b, 3, 0, 0, HALF, HALF),
        (high_a, 1, 0, 0, HALF, HALF),
    ]
    pieces += [(far_low, 2, 0, 0, 0, HALF), (far_high, 2, 0, 0, HALF, HALF)]
    placed, partial = place_early(where, hid, [], both(pieces, far_low, far_high))
    pieces = [
        (below_x, 3, 1, 0, 0, OWNED),
        (above_x, 1, 1, 0, 0, OWNED),
        (far_low_x, 2, 1, 0, 0, HALF),
        (far_high_x, 2, 1, 0, HALF, HALF),
    ]
    pieces = both(pieces, partial)
    return tuple(
        place_late(where, hid, partial, cosine, sine, cached, placed, pieces, steps, rows, [rows])
    )


def solution(mesh):
    return jax.shard_map(
        local,
        mesh=mesh,
        in_specs=(
            P(("rep", "tp"), None),
            P(None, "rep", "tp"),
            P(None, "rep", "tp"),
            P("rep", None, "tp"),
            P("rep", None, "tp"),
            P("rep"),
        ),
        out_specs=(P(None, "tp"), P(None, "rep", "tp"), P(None, "rep", "tp")),
        check_vma=False,
    )
```

```python
import math

import jax
import jax.numpy as jnp
from jax import lax
from jax.experimental import pallas as pl
from jax.experimental.pallas import tpu as pltpu
from jax.sharding import PartitionSpec as P

KVH = 8
HD = 128
QH = 128
GROUPS = QH // KVH
SCALE = HD ** (-0.5)

REP = 16
TP = 8
ROWS = 128
OWNED = TP * ROWS
HALF = OWNED // 2
COLS = 2 * HD
VMEM_BYTES = 60 * 2**20
CACHE_VMEM = 60 * 2**20
PLACE_VMEM = 48 * 2**20
PLACE_COST = pl.CostEstimate(flops=20000000000, bytes_accessed=1000, transcendentals=0)

rope_base = 500000.0

ANY = pl.BlockSpec(memory_space=pl.ANY)
HBM = pl.BlockSpec(memory_space=pltpu.HBM)
SMEM = pl.BlockSpec(memory_space=pltpu.SMEM)
VMEM = pl.BlockSpec(memory_space=pltpu.VMEM)


def z_shift(step):
    return [(r, ((((r >> 2) + step) % 4) << 2) | (r & 3)) for r in range(REP)]


X_SWAP = [(r, r ^ 2) for r in range(REP)]
CORE_SWAP = [(r, r ^ 1) for r in range(REP)]


def send(value, pairs):
    return lax.ppermute(value, "rep", pairs)


def scaled_frequencies(width):
    pair_index = jnp.arange(width // 2, dtype=jnp.float32)
    base_freq = rope_base ** (-2.0 * pair_index / width)
    wavelength = 2.0 * math.pi / base_freq
    smooth = (8192.0 / wavelength - 1.0) / 3.0
    blended = (1.0 - smooth) * base_freq / 8.0 + smooth * base_freq
    return jnp.where(
        wavelength < 2048.0, base_freq, jnp.where(wavelength > 8192.0, base_freq / 8.0, blended)
    )


def rotation_tables(lengths, steps):
    positions = lengths[None, :] + jnp.arange(steps, dtype=jnp.int32)[:, None]
    angles = positions.reshape(-1, 1).astype(jnp.float32) * scaled_frequencies(HD)
    cosine, sine = jnp.cos(angles), jnp.sin(angles)
    return (
        jnp.concatenate([cosine, cosine], axis=-1),
        jnp.concatenate([-sine, sine], axis=-1),
    )


def pack_kernel(kv_ref, hid_ref, out_ref):
    steps, _, width = hid_ref.shape
    flat = jnp.concatenate([hid_ref[s].astype(jnp.float32) for s in range(steps)], axis=0)
    cut = [flat[:, c : c + COLS] for c in range(0, width, COLS)]
    cut = jnp.concatenate(cut, axis=0).astype(jnp.bfloat16)
    for t in range(TP):
        out_ref[t, :ROWS] = kv_ref[:, t * COLS : (t + 1) * COLS].astype(jnp.bfloat16)
        out_ref[t, ROWS:] = cut


def pack(kv_master, hidden):
    return pl.pallas_call(
        pack_kernel,
        in_specs=[VMEM, VMEM],
        out_specs=VMEM,
        out_shape=jax.ShapeDtypeStruct((TP, ROWS + hidden.size // COLS, COLS), jnp.bfloat16),
        compiler_params=pltpu.CompilerParams(vmem_limit_bytes=VMEM_BYTES),
    )(kv_master, hidden)


def cache_kernel(first, count, len_ref, q_ref, k_ref, v_ref, q_out, acc_out, m_out, l_out, q_scr, s_scr):
    i = pl.program_id(0)
    steps, rows = q_ref.shape[0], q_ref.shape[1]
    span = k_ref.shape[1]
    chunk = 2048

    @pl.when(i == 0)
    def _():
        flat = jnp.concatenate([q_ref[s].astype(jnp.float32) for s in range(steps)], axis=0)
        for g in range(GROUPS):
            q_scr[pl.ds(g, steps * rows, stride=GROUPS), :] = flat[:, g * HD : (g + 1) * HD]
        q_out[...] = q_scr[...].reshape(q_out.shape).astype(q_out.dtype)

    b = first + i
    base = [pl.multiple_of((s * rows + b) * GROUPS, GROUPS) for s in range(steps)]
    q = jnp.concatenate([q_scr[pl.ds(o, GROUPS), :] for o in base], axis=0).astype(jnp.bfloat16)
    length = len_ref[b]
    top = jnp.full((steps * GROUPS, 1), -jnp.inf, jnp.float32)
    for c in range(span // chunk):
        keys = k_ref[0, c * chunk : (c + 1) * chunk, :]
        scores = (
            lax.dot_general(q, keys, (((1,), (1,)), ((), ())), preferred_element_type=jnp.float32)
            * SCALE
        )
        place = c * chunk + lax.broadcasted_iota(jnp.int32, scores.shape, 1)
        scores = jnp.where(place < length, scores, -jnp.inf)
        s_scr[:, c * chunk : (c + 1) * chunk] = scores
        top = jnp.maximum(top, jnp.max(scores, axis=-1, keepdims=True))
    total = jnp.zeros((steps * GROUPS, 1), jnp.float32)
    acc = jnp.zeros((steps * GROUPS, HD), jnp.float32)
    for c in range(span // chunk):
        weights = jnp.exp(s_scr[:, c * chunk : (c + 1) * chunk] - top)
        total = total + jnp.sum(weights, axis=-1, keepdims=True)
        acc = acc + jnp.dot(
            weights.astype(jnp.bfloat16),
            v_ref[0, c * chunk : (c + 1) * chunk, :],
            preferred_element_type=jnp.float32,
        )
    for s in range(steps):
        part = slice(s * GROUPS, (s + 1) * GROUPS)
        place = s * count + i
        acc_out[place] = acc[part]
        m_out[place] = jnp.broadcast_to(top[part], (GROUPS, HD))
        l_out[place] = jnp.broadcast_to(total[part], (GROUPS, HD))


def attend_cache(queries, key_cache, value_cache, lengths, first, count):
    steps, rows, width = queries.shape
    span = key_cache.shape[1]
    part = jax.ShapeDtypeStruct((steps * count, GROUPS, HD), jnp.float32)
    return pl.pallas_call(
        lambda *refs: cache_kernel(first, count, *refs),
        grid=(count,),
        in_specs=[
            SMEM,
            pl.BlockSpec((steps, rows, width), lambda i: (0, 0, 0)),
            pl.BlockSpec((1, span, HD), lambda i: (first + i, 0, 0)),
            pl.BlockSpec((1, span, HD), lambda i: (first + i, 0, 0)),
        ],
        out_specs=[pl.BlockSpec((steps * rows, GROUPS, HD), lambda i: (0, 0, 0))]
        + [pl.BlockSpec(part.shape, lambda i: (0, 0, 0))] * 3,
        out_shape=[jax.ShapeDtypeStruct((steps * rows, GROUPS, HD), jnp.bfloat16)] + [part] * 3,
        scratch_shapes=[
            pltpu.VMEM((steps * rows * GROUPS, HD), jnp.float32),
            pltpu.VMEM((steps * GROUPS, span), jnp.float32),
        ],
        compiler_params=pltpu.CompilerParams(vmem_limit_bytes=CACHE_VMEM),
        cost_estimate=pl.CostEstimate(
            flops=4 * count * steps * GROUPS * span * HD,
            bytes_accessed=4 * count * span * HD,
            transcendentals=count * steps * GROUPS * span,
        ),
    )(lengths, queries, key_cache, value_cache)


def place_pieces(spots, where_ref, moved_ref, piece_refs, out_ref, buf, hid, in_sem, out_sem):
    rep = where_ref[0]
    hidden_in = pltpu.make_async_copy(moved_ref.at[:, pl.ds(ROWS, hid.shape[1])], hid, in_sem.at[len(spots)])
    hidden_in.start()
    owners, reads, writes, offset = [], [], [], 0
    for i, (dz, dx, dc, first, count) in enumerate(spots):
        owner = ((((rep >> 2) + dz) & 3) << 2) | ((rep & 3) ^ (2 * dx + dc))
        start = pl.multiple_of(owner * OWNED + first, ROWS)
        read = pltpu.make_async_copy(piece_refs[i], buf.at[pl.ds(offset, count)], in_sem.at[i])
        write = pltpu.make_async_copy(
            buf.at[pl.ds(offset, count)], out_ref.at[pl.ds(start, count)], out_sem.at[i]
        )
        read.start()
        owners.append(owner)
        reads.append(read)
        writes.append(write)
        offset += count
    hidden_in.wait()
    line = hid.shape[1] // (2 * OWNED // COLS)
    total, offset = jnp.zeros((line, COLS), jnp.float32), 0
    for owner, read, write, (_, _, _, first, count) in zip(owners, reads, writes, spots):
        rows = pl.ds(pl.multiple_of((owner & 1) * (OWNED // COLS * line), 16), OWNED // COLS * line)
        cut = hid[owner >> 1, rows, :].astype(jnp.float32)
        cut = [cut[c * line : (c + 1) * line] for c in range(first // COLS, (first + count) // COLS)]
        cut = jnp.concatenate(cut, axis=1).astype(jnp.bfloat16)
        read.wait()
        write.start()
        total = total + jnp.dot(
            cut, buf[offset : offset + count, :], preferred_element_type=jnp.float32
        )
        offset += count
    return total, writes


def early_kernel(spots, follows, where_ref, moved_ref, *refs):
    if follows:
        before_ref, _, *refs = refs
    count = len(spots)
    out_ref, sum_ref, *work = refs[count:]
    total, writes = place_pieces(spots, where_ref, moved_ref, refs[:count], out_ref, *work)
    sum_ref[...] = total + before_ref[...] if follows else total
    for write in writes:
        write.wait()


def late_kernel(spots, steps, rows, groups, where_ref, moved_ref, sum_ref, cos_ref, sin_ref, *refs):
    cached = [refs[4 * i : 4 * i + 4] for i in range(len(groups))]
    refs = refs[4 * len(groups) + 1 :]
    count = len(spots)
    out_ref, kv_ref, att_ref, turn, *work = refs[count:]
    total, writes = place_pieces(spots, where_ref, moved_ref, refs[:count], out_ref, *work)
    heads = steps * rows * GROUPS

    def join(which):
        return jnp.concatenate(
            [
                group[which][s * n : (s + 1) * n].reshape(n * GROUPS, HD)
                for s in range(steps)
                for group, n in zip(cached, groups)
            ],
            axis=0,
        )

    acc, old_top, old_total = join(1), join(2)[:, :1], join(3)[:, :1]
    total = total + sum_ref[...]
    keys = total[:, :HD]
    keys = keys * cos_ref[...] + pltpu.roll(keys, HD // 2, 1) * sin_ref[...]
    keys = keys.astype(jnp.bfloat16)
    values = total[:, HD:].astype(jnp.bfloat16)
    for s in range(steps):
        kv_ref[s, :, :HD] = keys[s * rows : (s + 1) * rows]
        kv_ref[s, :, HD:] = values[s * rows : (s + 1) * rows]
    scores = (
        lax.dot_general(
            cached[0][0][...].reshape(heads, HD),
            keys,
            (((1,), (1,)), ((), ())),
            preferred_element_type=jnp.float32,
        )
        * SCALE
    )
    line = lax.broadcasted_iota(jnp.int32, scores.shape, 0) // GROUPS
    column = lax.broadcasted_iota(jnp.int32, scores.shape, 1)
    seen = (line % rows == column % rows) & (column // rows <= line // rows)
    scores = jnp.where(seen, scores, -jnp.inf)
    top = jnp.maximum(old_top, jnp.max(scores, axis=-1, keepdims=True))
    fresh = jnp.exp(scores - top)
    fade = jnp.exp(old_top - top)
    denominator = old_total * fade + jnp.sum(fresh, axis=-1, keepdims=True)
    mixed = acc * (fade / denominator) + jnp.dot(
        (fresh / denominator).astype(jnp.bfloat16), values, preferred_element_type=jnp.float32
    )
    turn[...] = mixed
    for g in range(GROUPS):
        head = turn[pl.ds(g, steps * rows, stride=GROUPS), :].astype(jnp.bfloat16)
        for s in range(steps):
            att_ref[s, :, g * HD : (g + 1) * HD] = head[s * rows : (s + 1) * rows]
    for write in writes:
        write.wait()


def scratch(spots, moved):
    return [
        pltpu.VMEM((sum(s[4] for s in spots), COLS), jnp.bfloat16),
        pltpu.VMEM((TP, moved.shape[1] - ROWS, COLS), jnp.bfloat16),
        pltpu.SemaphoreType.DMA((len(spots) + 1,)),
        pltpu.SemaphoreType.DMA((len(spots),)),
    ]


def place_early(where, moved, before, pieces):
    spots = [p[1:] for p in pieces]
    lines = (moved.shape[1] - ROWS) * COLS // (2 * OWNED)
    return pl.pallas_call(
        lambda *refs: early_kernel(spots, bool(before), *refs),
        in_specs=[SMEM, ANY] + [VMEM, ANY][: len(before)] + [HBM] * len(pieces),
        out_specs=[ANY, VMEM],
        out_shape=[
            jax.ShapeDtypeStruct((REP * OWNED, COLS), jnp.bfloat16),
            jax.ShapeDtypeStruct((lines, COLS), jnp.float32),
        ],
        scratch_shapes=scratch(spots, moved),
        input_output_aliases={3: 0} if before else {},
        compiler_params=pltpu.CompilerParams(vmem_limit_bytes=PLACE_VMEM),
        cost_estimate=PLACE_COST,
    )(where, moved, *before, *[p[0] for p in pieces])


def place_late(where, moved, partial, cosine, sine, cached, placed, pieces, steps, rows, groups):
    spots = [p[1:] for p in pieces]
    small = 3 + 4 * len(groups)
    return pl.pallas_call(
        lambda *refs: late_kernel(spots, steps, rows, groups, *refs),
        in_specs=[SMEM, ANY] + [VMEM] * small + [ANY] + [HBM] * len(pieces),
        out_specs=[ANY, VMEM, VMEM],
        out_shape=[
            jax.ShapeDtypeStruct((REP * OWNED, COLS), jnp.bfloat16),
            jax.ShapeDtypeStruct((steps, rows, COLS), jnp.bfloat16),
            jax.ShapeDtypeStruct((steps, rows, GROUPS * HD), jnp.bfloat16),
        ],
        scratch_shapes=[
            pltpu.VMEM((steps * rows * GROUPS, HD), jnp.float32),
            *scratch(spots, moved),
        ],
        input_output_aliases={2 + small: 0},
        compiler_params=pltpu.CompilerParams(vmem_limit_bytes=PLACE_VMEM),
        cost_estimate=PLACE_COST,
    )(where, moved, partial, cosine, sine, *cached, placed, *[p[0] for p in pieces])


def exchange(pieces, *behind):
    held = lax.optimization_barrier(tuple(p[0] for p in pieces) + behind)
    pieces = [(v, *p[1:]) for v, p in zip(held, pieces)]
    other = [(send(p[0], CORE_SWAP), p[1], p[2], 1, p[4], p[5]) for p in pieces]
    return (pieces, other, *held[len(pieces) :])


def local(kv_master, hidden, queries, key_cache, value_cache, lengths):
    steps, rows, _ = hidden.shape
    where = lax.axis_index("rep").astype(jnp.int32).reshape(1)

    moved = lax.all_to_all(pack(kv_master, hidden), "tp", split_axis=0, concat_axis=0, tiled=True)
    owned = moved[:, :ROWS]
    cosine, sine = rotation_tables(lengths, steps)
    cached = attend_cache(queries, key_cache, value_cache, lengths, 0, rows)
    low, high = owned[: TP // 2].reshape(HALF, COLS), owned[TP // 2 :].reshape(HALF, COLS)
    owned, low, high, *cached = lax.optimization_barrier((owned, low, high, *cached))
    owned = owned.reshape(OWNED, COLS)

    up, down = z_shift(1), z_shift(-1)
    low_b, high_a = send(low, up), send(high, down)
    low_a, high_b = send(low, down), send(high, up)
    near_x = send(owned, X_SWAP)
    low_b, high_a, cosine, sine = lax.optimization_barrier((low_b, high_a, cosine, sine))
    below_x, above_x = send(near_x, up), send(near_x, down)
    far_low, far_high = send(low_b, up), send(high_a, down)
    far_low_x, far_high_x = send(far_low, X_SWAP), send(far_high, X_SWAP)

    near = [
        (owned, 0, 0, 0, 0, OWNED),
        (near_x, 0, 1, 0, 0, OWNED),
        (low_b, 3, 0, 0, 0, HALF),
        (high_a, 1, 0, 0, HALF, HALF),
        (low_a, 1, 0, 0, 0, HALF),
        (high_b, 3, 0, 0, HALF, HALF),
    ]
    far = [(far_low, 2, 0, 0, 0, HALF), (far_high, 2, 0, 0, HALF, HALF)]
    near, near_other = exchange(near)
    far, far_other = exchange(far)
    pieces = near + far + near_other + far_other
    placed, partial = place_early(where, moved, [], pieces)
    last = [
        (below_x, 3, 1, 0, 0, OWNED),
        (above_x, 1, 1, 0, 0, OWNED),
        (far_low_x, 2, 1, 0, 0, HALF),
        (far_high_x, 2, 1, 0, HALF, HALF),
    ]
    last, last_other, partial = exchange(last, partial)
    placed, partial = place_early(where, moved, [partial, placed], last)
    return tuple(
        place_late(
            where, moved, partial, cosine, sine, cached, placed, last_other, steps, rows, [rows]
        )
    )


def solution(mesh):
    return jax.shard_map(
        local,
        mesh=mesh,
        in_specs=(
            P(("rep", "tp"), None),
            P(None, "rep", "tp"),
            P(None, "rep", "tp"),
            P("rep", None, "tp"),
            P("rep", None, "tp"),
            P("rep"),
        ),
        out_specs=(P(None, "tp"), P(None, "rep", "tp"), P(None, "rep", "tp")),
        check_vma=False,
    )
```

```python
import math

import jax
import jax.numpy as jnp
from jax import lax
from jax.experimental import pallas as pl
from jax.experimental.pallas import tpu as pltpu
from jax.sharding import PartitionSpec as P

KVH = 8
HD = 128
QH = 128
GROUPS = QH // KVH
SCALE = HD ** (-0.5)

REP = 16
TP = 8
ROWS = 128
OWNED = TP * ROWS
HALF = OWNED // 2
COLS = 2 * HD
VMEM_BYTES = 60 * 2**20
CACHE_VMEM = 60 * 2**20
PLACE_VMEM = 48 * 2**20
PLACE_COST = pl.CostEstimate(flops=20000000000, bytes_accessed=1000, transcendentals=0)

rope_base = 500000.0

ANY = pl.BlockSpec(memory_space=pl.ANY)
HBM = pl.BlockSpec(memory_space=pltpu.HBM)
SMEM = pl.BlockSpec(memory_space=pltpu.SMEM)
VMEM = pl.BlockSpec(memory_space=pltpu.VMEM)


def z_shift(step):
    return [(r, ((((r >> 2) + step) % 4) << 2) | (r & 3)) for r in range(REP)]


X_SWAP = [(r, r ^ 2) for r in range(REP)]
CORE_SWAP = [(r, r ^ 1) for r in range(REP)]


def send(value, pairs):
    return lax.ppermute(value, "rep", pairs)


def scaled_frequencies(width):
    pair_index = jnp.arange(width // 2, dtype=jnp.float32)
    base_freq = rope_base ** (-2.0 * pair_index / width)
    wavelength = 2.0 * math.pi / base_freq
    smooth = (8192.0 / wavelength - 1.0) / 3.0
    blended = (1.0 - smooth) * base_freq / 8.0 + smooth * base_freq
    return jnp.where(
        wavelength < 2048.0, base_freq, jnp.where(wavelength > 8192.0, base_freq / 8.0, blended)
    )


def rotation_tables(lengths, steps):
    positions = lengths[None, :] + jnp.arange(steps, dtype=jnp.int32)[:, None]
    angles = positions.reshape(-1, 1).astype(jnp.float32) * scaled_frequencies(HD)
    cosine, sine = jnp.cos(angles), jnp.sin(angles)
    return (
        jnp.concatenate([cosine, cosine], axis=-1),
        jnp.concatenate([-sine, sine], axis=-1),
    )


def pack_kernel(kv_ref, hid_ref, out_ref):
    steps, _, width = hid_ref.shape
    flat = jnp.concatenate([hid_ref[s].astype(jnp.float32) for s in range(steps)], axis=0)
    cut = [flat[:, c : c + COLS] for c in range(0, width, COLS)]
    cut = jnp.concatenate(cut, axis=0).astype(jnp.bfloat16)
    for t in range(TP):
        out_ref[t, :ROWS] = kv_ref[:, t * COLS : (t + 1) * COLS].astype(jnp.bfloat16)
        out_ref[t, ROWS:] = cut


def pack(kv_master, hidden):
    return pl.pallas_call(
        pack_kernel,
        in_specs=[VMEM, VMEM],
        out_specs=VMEM,
        out_shape=jax.ShapeDtypeStruct((TP, ROWS + hidden.size // COLS, COLS), jnp.bfloat16),
        compiler_params=pltpu.CompilerParams(vmem_limit_bytes=VMEM_BYTES),
    )(kv_master, hidden)


def cache_kernel(first, count, len_ref, q_ref, k_ref, v_ref, q_out, acc_out, m_out, l_out, q_scr, s_scr):
    i = pl.program_id(0)
    steps, rows = q_ref.shape[0], q_ref.shape[1]
    span = k_ref.shape[1]
    chunk = 2048

    @pl.when(i == 0)
    def _():
        flat = jnp.concatenate([q_ref[s].astype(jnp.float32) for s in range(steps)], axis=0)
        for g in range(GROUPS):
            q_scr[pl.ds(g, steps * rows, stride=GROUPS), :] = flat[:, g * HD : (g + 1) * HD]
        q_out[...] = q_scr[...].reshape(q_out.shape).astype(q_out.dtype)

    b = first + i
    base = [pl.multiple_of((s * rows + b) * GROUPS, GROUPS) for s in range(steps)]
    q = jnp.concatenate([q_scr[pl.ds(o, GROUPS), :] for o in base], axis=0).astype(jnp.bfloat16)
    length = len_ref[b]
    top = jnp.full((steps * GROUPS, 1), -jnp.inf, jnp.float32)
    for c in range(span // chunk):
        keys = k_ref[0, c * chunk : (c + 1) * chunk, :]
        scores = (
            lax.dot_general(q, keys, (((1,), (1,)), ((), ())), preferred_element_type=jnp.float32)
            * SCALE
        )
        place = c * chunk + lax.broadcasted_iota(jnp.int32, scores.shape, 1)
        scores = jnp.where(place < length, scores, -jnp.inf)
        s_scr[:, c * chunk : (c + 1) * chunk] = scores
        top = jnp.maximum(top, jnp.max(scores, axis=-1, keepdims=True))
    total = jnp.zeros((steps * GROUPS, 1), jnp.float32)
    acc = jnp.zeros((steps * GROUPS, HD), jnp.float32)
    for c in range(span // chunk):
        weights = jnp.exp(s_scr[:, c * chunk : (c + 1) * chunk] - top)
        total = total + jnp.sum(weights, axis=-1, keepdims=True)
        acc = acc + jnp.dot(
            weights.astype(jnp.bfloat16),
            v_ref[0, c * chunk : (c + 1) * chunk, :],
            preferred_element_type=jnp.float32,
        )
    for s in range(steps):
        part = slice(s * GROUPS, (s + 1) * GROUPS)
        place = s * count + i
        acc_out[place] = acc[part]
        m_out[place] = jnp.broadcast_to(top[part], (GROUPS, HD))
        l_out[place] = jnp.broadcast_to(total[part], (GROUPS, HD))


def attend_cache(queries, key_cache, value_cache, lengths, first, count):
    steps, rows, width = queries.shape
    span = key_cache.shape[1]
    part = jax.ShapeDtypeStruct((steps * count, GROUPS, HD), jnp.float32)
    return pl.pallas_call(
        lambda *refs: cache_kernel(first, count, *refs),
        grid=(count,),
        in_specs=[
            SMEM,
            pl.BlockSpec((steps, rows, width), lambda i: (0, 0, 0)),
            pl.BlockSpec((1, span, HD), lambda i: (first + i, 0, 0)),
            pl.BlockSpec((1, span, HD), lambda i: (first + i, 0, 0)),
        ],
        out_specs=[pl.BlockSpec((steps * rows, GROUPS, HD), lambda i: (0, 0, 0))]
        + [pl.BlockSpec(part.shape, lambda i: (0, 0, 0))] * 3,
        out_shape=[jax.ShapeDtypeStruct((steps * rows, GROUPS, HD), jnp.bfloat16)] + [part] * 3,
        scratch_shapes=[
            pltpu.VMEM((steps * rows * GROUPS, HD), jnp.float32),
            pltpu.VMEM((steps * GROUPS, span), jnp.float32),
        ],
        compiler_params=pltpu.CompilerParams(vmem_limit_bytes=CACHE_VMEM),
        cost_estimate=pl.CostEstimate(
            flops=4 * count * steps * GROUPS * span * HD,
            bytes_accessed=4 * count * span * HD,
            transcendentals=count * steps * GROUPS * span,
        ),
    )(lengths, queries, key_cache, value_cache)


def place_pieces(spots, where_ref, moved_ref, piece_refs, out_ref, buf, hid, in_sem, out_sem, meanwhile=tuple):
    rep = where_ref[0]
    hidden_in = pltpu.make_async_copy(moved_ref.at[:, pl.ds(ROWS, hid.shape[1])], hid, in_sem.at[len(spots)])
    hidden_in.start()
    owners, reads, writes, offset = [], [], [], 0
    for i, (dz, dx, dc, first, count) in enumerate(spots):
        owner = ((((rep >> 2) + dz) & 3) << 2) | ((rep & 3) ^ (2 * dx + dc))
        start = pl.multiple_of(owner * OWNED + first, ROWS)
        read = pltpu.make_async_copy(piece_refs[i], buf.at[pl.ds(offset, count)], in_sem.at[i])
        write = pltpu.make_async_copy(
            buf.at[pl.ds(offset, count)], out_ref.at[pl.ds(start, count)], out_sem.at[i]
        )
        read.start()
        owners.append(owner)
        reads.append(read)
        writes.append(write)
        offset += count
    ready = meanwhile()
    hidden_in.wait()
    line = hid.shape[1] // (2 * OWNED // COLS)
    total, offset = jnp.zeros((line, COLS), jnp.float32), 0
    for owner, read, write, (_, _, _, first, count) in zip(owners, reads, writes, spots):
        rows = pl.ds(pl.multiple_of((owner & 1) * (OWNED // COLS * line), 16), OWNED // COLS * line)
        cut = hid[owner >> 1, rows, :].astype(jnp.float32)
        cut = [cut[c * line : (c + 1) * line] for c in range(first // COLS, (first + count) // COLS)]
        cut = jnp.concatenate(cut, axis=1).astype(jnp.bfloat16)
        read.wait()
        write.start()
        total = total + jnp.dot(
            cut, buf[offset : offset + count, :], preferred_element_type=jnp.float32
        )
        offset += count
    return total, writes, ready


def early_kernel(spots, follows, where_ref, moved_ref, *refs):
    if follows:
        before_ref, _, *refs = refs
    count = len(spots)
    out_ref, sum_ref, *work = refs[count:]
    total, writes, _ = place_pieces(spots, where_ref, moved_ref, refs[:count], out_ref, *work)
    sum_ref[...] = total + before_ref[...] if follows else total
    for write in writes:
        write.wait()


def late_kernel(spots, steps, rows, groups, where_ref, moved_ref, sum_ref, cos_ref, sin_ref, *refs):
    cached = [refs[4 * i : 4 * i + 4] for i in range(len(groups))]
    refs = refs[4 * len(groups) + 1 :]
    count = len(spots)
    out_ref, kv_ref, att_ref, turn, *work = refs[count:]
    heads = steps * rows * GROUPS

    def join(which):
        return jnp.concatenate(
            [
                group[which][s * n : (s + 1) * n].reshape(n * GROUPS, HD)
                for s in range(steps)
                for group, n in zip(cached, groups)
            ],
            axis=0,
        )

    def meanwhile():
        return join(1), join(2)[:, :1], join(3)[:, :1], sum_ref[...], cos_ref[...], sin_ref[...]

    total, writes, ready = place_pieces(
        spots, where_ref, moved_ref, refs[:count], out_ref, *work, meanwhile
    )
    acc, old_top, old_total, before, cosine, sine = ready
    total = total + before
    keys = total[:, :HD]
    keys = keys * cosine + pltpu.roll(keys, HD // 2, 1) * sine
    keys = keys.astype(jnp.bfloat16)
    values = total[:, HD:].astype(jnp.bfloat16)
    for s in range(steps):
        kv_ref[s, :, :HD] = keys[s * rows : (s + 1) * rows]
        kv_ref[s, :, HD:] = values[s * rows : (s + 1) * rows]
    scores = (
        lax.dot_general(
            cached[0][0][...].reshape(heads, HD),
            keys,
            (((1,), (1,)), ((), ())),
            preferred_element_type=jnp.float32,
        )
        * SCALE
    )
    line = lax.broadcasted_iota(jnp.int32, scores.shape, 0) // GROUPS
    column = lax.broadcasted_iota(jnp.int32, scores.shape, 1)
    seen = (line % rows == column % rows) & (column // rows <= line // rows)
    scores = jnp.where(seen, scores, -jnp.inf)
    top = jnp.maximum(old_top, jnp.max(scores, axis=-1, keepdims=True))
    fresh = jnp.exp(scores - top)
    fade = jnp.exp(old_top - top)
    denominator = old_total * fade + jnp.sum(fresh, axis=-1, keepdims=True)
    mixed = acc * (fade / denominator) + jnp.dot(
        (fresh / denominator).astype(jnp.bfloat16), values, preferred_element_type=jnp.float32
    )
    turn[...] = mixed
    for g in range(GROUPS):
        head = turn[pl.ds(g, steps * rows, stride=GROUPS), :].astype(jnp.bfloat16)
        for s in range(steps):
            att_ref[s, :, g * HD : (g + 1) * HD] = head[s * rows : (s + 1) * rows]
    for write in writes:
        write.wait()


def scratch(spots, moved):
    return [
        pltpu.VMEM((sum(s[4] for s in spots), COLS), jnp.bfloat16),
        pltpu.VMEM((TP, moved.shape[1] - ROWS, COLS), jnp.bfloat16),
        pltpu.SemaphoreType.DMA((len(spots) + 1,)),
        pltpu.SemaphoreType.DMA((len(spots),)),
    ]


def place_early(where, moved, before, pieces):
    spots = [p[1:] for p in pieces]
    lines = (moved.shape[1] - ROWS) * COLS // (2 * OWNED)
    return pl.pallas_call(
        lambda *refs: early_kernel(spots, bool(before), *refs),
        in_specs=[SMEM, ANY] + [VMEM, ANY][: len(before)] + [HBM] * len(pieces),
        out_specs=[ANY, VMEM],
        out_shape=[
            jax.ShapeDtypeStruct((REP * OWNED, COLS), jnp.bfloat16),
            jax.ShapeDtypeStruct((lines, COLS), jnp.float32),
        ],
        scratch_shapes=scratch(spots, moved),
        input_output_aliases={3: 0} if before else {},
        compiler_params=pltpu.CompilerParams(vmem_limit_bytes=PLACE_VMEM),
        cost_estimate=PLACE_COST,
    )(where, moved, *before, *[p[0] for p in pieces])


def place_late(where, moved, partial, cosine, sine, cached, placed, pieces, steps, rows, groups):
    spots = [p[1:] for p in pieces]
    small = 3 + 4 * len(groups)
    return pl.pallas_call(
        lambda *refs: late_kernel(spots, steps, rows, groups, *refs),
        in_specs=[SMEM, ANY] + [VMEM] * small + [ANY] + [HBM] * len(pieces),
        out_specs=[ANY, VMEM, VMEM],
        out_shape=[
            jax.ShapeDtypeStruct((REP * OWNED, COLS), jnp.bfloat16),
            jax.ShapeDtypeStruct((steps, rows, COLS), jnp.bfloat16),
            jax.ShapeDtypeStruct((steps, rows, GROUPS * HD), jnp.bfloat16),
        ],
        scratch_shapes=[
            pltpu.VMEM((steps * rows * GROUPS, HD), jnp.float32),
            *scratch(spots, moved),
        ],
        input_output_aliases={2 + small: 0},
        compiler_params=pltpu.CompilerParams(vmem_limit_bytes=PLACE_VMEM),
        cost_estimate=PLACE_COST,
    )(where, moved, partial, cosine, sine, *cached, placed, *[p[0] for p in pieces])


def exchange(pieces, *behind):
    held = lax.optimization_barrier(tuple(p[0] for p in pieces) + behind)
    pieces = [(v, *p[1:]) for v, p in zip(held, pieces)]
    other = [(send(p[0], CORE_SWAP), p[1], p[2], 1, p[4], p[5]) for p in pieces]
    return (pieces, other, *held[len(pieces) :])


def local(kv_master, hidden, queries, key_cache, value_cache, lengths):
    steps, rows, _ = hidden.shape
    where = lax.axis_index("rep").astype(jnp.int32).reshape(1)

    moved = lax.all_to_all(pack(kv_master, hidden), "tp", split_axis=0, concat_axis=0, tiled=True)
    owned = moved[:, :ROWS]
    cosine, sine = rotation_tables(lengths, steps)
    cached = attend_cache(queries, key_cache, value_cache, lengths, 0, rows)
    low, high = owned[: TP // 2].reshape(HALF, COLS), owned[TP // 2 :].reshape(HALF, COLS)
    owned, low, high, *cached = lax.optimization_barrier((owned, low, high, *cached))
    owned = owned.reshape(OWNED, COLS)

    up, down = z_shift(1), z_shift(-1)
    low_a, high_b = send(low, down), send(high, up)
    low_b, high_a = send(low, up), send(high, down)
    near_x = send(owned, X_SWAP)
    low_b, high_a, cosine, sine = lax.optimization_barrier((low_b, high_a, cosine, sine))
    below_x, above_x = send(near_x, up), send(near_x, down)
    far_low, far_high = send(low_b, up), send(high_a, down)
    far_low_x, far_high_x = send(far_low, X_SWAP), send(far_high, X_SWAP)

    near = [
        (owned, 0, 0, 0, 0, OWNED),
        (near_x, 0, 1, 0, 0, OWNED),
        (low_b, 3, 0, 0, 0, HALF),
        (high_a, 1, 0, 0, HALF, HALF),
        (low_a, 1, 0, 0, 0, HALF),
        (high_b, 3, 0, 0, HALF, HALF),
    ]
    far = [(far_low, 2, 0, 0, 0, HALF), (far_high, 2, 0, 0, HALF, HALF)]
    near, near_other = exchange(near)
    far, far_other = exchange(far)
    pieces = near + far + near_other + far_other
    placed, partial = place_early(where, moved, [], pieces)
    last = [
        (below_x, 3, 1, 0, 0, OWNED),
        (above_x, 1, 1, 0, 0, OWNED),
        (far_low_x, 2, 1, 0, 0, HALF),
        (far_high_x, 2, 1, 0, HALF, HALF),
    ]
    last, last_other, partial = exchange(last, partial)
    placed, partial = place_early(where, moved, [partial, placed], last)
    return tuple(
        place_late(
            where, moved, partial, cosine, sine, cached, placed, last_other, steps, rows, [rows]
        )
    )


def solution(mesh):
    return jax.shard_map(
        local,
        mesh=mesh,
        in_specs=(
            P(("rep", "tp"), None),
            P(None, "rep", "tp"),
            P(None, "rep", "tp"),
            P("rep", None, "tp"),
            P("rep", None, "tp"),
            P("rep"),
        ),
        out_specs=(P(None, "tp"), P(None, "rep", "tp"), P(None, "rep", "tp")),
        check_vma=False,
    )
```

```python
import math

import jax
import jax.numpy as jnp
from jax import lax
from jax.experimental import pallas as pl
from jax.experimental.pallas import tpu as pltpu
from jax.sharding import PartitionSpec as P

KVH = 8
HD = 128
QH = 128
GROUPS = QH // KVH
SCALE = HD ** (-0.5)

REP = 16
TP = 8
ROWS = 128
OWNED = TP * ROWS
HALF = OWNED // 2
COLS = 2 * HD
VMEM_BYTES = 60 * 2**20
PACK_STEPS = 2
CACHE_VMEM = 60 * 2**20
PLACE_VMEM = 48 * 2**20
PLACE_COST = pl.CostEstimate(flops=20000000000, bytes_accessed=1000, transcendentals=0)

rope_base = 500000.0

ANY = pl.BlockSpec(memory_space=pl.ANY)
HBM = pl.BlockSpec(memory_space=pltpu.HBM)
SMEM = pl.BlockSpec(memory_space=pltpu.SMEM)
VMEM = pl.BlockSpec(memory_space=pltpu.VMEM)


def z_shift(step):
    return [(r, ((((r >> 2) + step) % 4) << 2) | (r & 3)) for r in range(REP)]


X_SWAP = [(r, r ^ 2) for r in range(REP)]
CORE_SWAP = [(r, r ^ 1) for r in range(REP)]


def send(value, pairs):
    return lax.ppermute(value, "rep", pairs)


def scaled_frequencies(width):
    pair_index = jnp.arange(width // 2, dtype=jnp.float32)
    base_freq = rope_base ** (-2.0 * pair_index / width)
    wavelength = 2.0 * math.pi / base_freq
    smooth = (8192.0 / wavelength - 1.0) / 3.0
    blended = (1.0 - smooth) * base_freq / 8.0 + smooth * base_freq
    return jnp.where(
        wavelength < 2048.0, base_freq, jnp.where(wavelength > 8192.0, base_freq / 8.0, blended)
    )


def rotation_tables(lengths, steps):
    positions = lengths[None, :] + jnp.arange(steps, dtype=jnp.int32)[:, None]
    angles = positions.reshape(-1, 1).astype(jnp.float32) * scaled_frequencies(HD)
    cosine, sine = jnp.cos(angles), jnp.sin(angles)
    return (
        jnp.concatenate([cosine, cosine], axis=-1),
        jnp.concatenate([-sine, sine], axis=-1),
    )


def pack_kernel(kv_ref, hid_ref, out_ref):
    steps, _, width = hid_ref.shape
    flat = jnp.concatenate([hid_ref[s].astype(jnp.float32) for s in range(steps)], axis=0)
    cut = [flat[:, c : c + COLS] for c in range(0, width, COLS)]
    cut = jnp.concatenate(cut, axis=0).astype(jnp.bfloat16)
    for t in range(out_ref.shape[0]):
        out_ref[t, :ROWS] = kv_ref[:, t * COLS : (t + 1) * COLS].astype(jnp.bfloat16)
        out_ref[t, ROWS:] = cut


def pack(kv_master, hidden):
    shape = (TP, ROWS + hidden.size // COLS, COLS)
    return pl.pallas_call(
        pack_kernel,
        grid=(PACK_STEPS,),
        in_specs=[
            pl.BlockSpec((ROWS, TP * COLS // PACK_STEPS), lambda i: (0, i)),
            pl.BlockSpec(hidden.shape, lambda i: (0, 0, 0)),
        ],
        out_specs=pl.BlockSpec((TP // PACK_STEPS, *shape[1:]), lambda i: (i, 0, 0)),
        out_shape=jax.ShapeDtypeStruct(shape, jnp.bfloat16),
        compiler_params=pltpu.CompilerParams(vmem_limit_bytes=VMEM_BYTES),
    )(kv_master, hidden)


def cache_kernel(first, count, len_ref, q_ref, k_ref, v_ref, q_out, acc_out, m_out, l_out, q_scr, s_scr):
    i = pl.program_id(0)
    steps, rows = q_ref.shape[0], q_ref.shape[1]
    span = k_ref.shape[1]
    chunk = 2048

    @pl.when(i == 0)
    def _():
        flat = jnp.concatenate([q_ref[s].astype(jnp.float32) for s in range(steps)], axis=0)
        for g in range(GROUPS):
            q_scr[pl.ds(g, steps * rows, stride=GROUPS), :] = flat[:, g * HD : (g + 1) * HD]
        q_out[...] = q_scr[...].reshape(q_out.shape).astype(q_out.dtype)

    b = first + i
    base = [pl.multiple_of((s * rows + b) * GROUPS, GROUPS) for s in range(steps)]
    q = jnp.concatenate([q_scr[pl.ds(o, GROUPS), :] for o in base], axis=0).astype(jnp.bfloat16)
    length = len_ref[b]
    top = jnp.full((steps * GROUPS, 1), -jnp.inf, jnp.float32)
    for c in range(span // chunk):
        keys = k_ref[0, c * chunk : (c + 1) * chunk, :]
        scores = (
            lax.dot_general(q, keys, (((1,), (1,)), ((), ())), preferred_element_type=jnp.float32)
            * SCALE
        )
        place = c * chunk + lax.broadcasted_iota(jnp.int32, scores.shape, 1)
        scores = jnp.where(place < length, scores, -jnp.inf)
        s_scr[:, c * chunk : (c + 1) * chunk] = scores
        top = jnp.maximum(top, jnp.max(scores, axis=-1, keepdims=True))
    total = jnp.zeros((steps * GROUPS, 1), jnp.float32)
    acc = jnp.zeros((steps * GROUPS, HD), jnp.float32)
    for c in range(span // chunk):
        weights = jnp.exp(s_scr[:, c * chunk : (c + 1) * chunk] - top)
        total = total + jnp.sum(weights, axis=-1, keepdims=True)
        acc = acc + jnp.dot(
            weights.astype(jnp.bfloat16),
            v_ref[0, c * chunk : (c + 1) * chunk, :],
            preferred_element_type=jnp.float32,
        )
    for s in range(steps):
        part = slice(s * GROUPS, (s + 1) * GROUPS)
        place = s * count + i
        acc_out[place] = acc[part]
        m_out[place] = jnp.broadcast_to(top[part], (GROUPS, HD))
        l_out[place] = jnp.broadcast_to(total[part], (GROUPS, HD))


def attend_cache(queries, key_cache, value_cache, lengths, first, count):
    steps, rows, width = queries.shape
    span = key_cache.shape[1]
    part = jax.ShapeDtypeStruct((steps * count, GROUPS, HD), jnp.float32)
    return pl.pallas_call(
        lambda *refs: cache_kernel(first, count, *refs),
        grid=(count,),
        in_specs=[
            SMEM,
            pl.BlockSpec((steps, rows, width), lambda i: (0, 0, 0)),
            pl.BlockSpec((1, span, HD), lambda i: (first + i, 0, 0)),
            pl.BlockSpec((1, span, HD), lambda i: (first + i, 0, 0)),
        ],
        out_specs=[pl.BlockSpec((steps * rows, GROUPS, HD), lambda i: (0, 0, 0))]
        + [pl.BlockSpec(part.shape, lambda i: (0, 0, 0))] * 3,
        out_shape=[jax.ShapeDtypeStruct((steps * rows, GROUPS, HD), jnp.bfloat16)] + [part] * 3,
        scratch_shapes=[
            pltpu.VMEM((steps * rows * GROUPS, HD), jnp.float32),
            pltpu.VMEM((steps * GROUPS, span), jnp.float32),
        ],
        compiler_params=pltpu.CompilerParams(vmem_limit_bytes=CACHE_VMEM),
        cost_estimate=pl.CostEstimate(
            flops=4 * count * steps * GROUPS * span * HD,
            bytes_accessed=4 * count * span * HD,
            transcendentals=count * steps * GROUPS * span,
        ),
    )(lengths, queries, key_cache, value_cache)


def place_pieces(spots, where_ref, moved_ref, piece_refs, out_ref, buf, hid, in_sem, out_sem, meanwhile=tuple):
    rep = where_ref[0]
    hidden_in = pltpu.make_async_copy(moved_ref.at[:, pl.ds(ROWS, hid.shape[1])], hid, in_sem.at[len(spots)])
    hidden_in.start()
    owners, reads, writes, offset = [], [], [], 0
    for i, (dz, dx, dc, first, count) in enumerate(spots):
        owner = ((((rep >> 2) + dz) & 3) << 2) | ((rep & 3) ^ (2 * dx + dc))
        start = pl.multiple_of(owner * OWNED + first, ROWS)
        read = pltpu.make_async_copy(piece_refs[i], buf.at[pl.ds(offset, count)], in_sem.at[i])
        write = pltpu.make_async_copy(
            buf.at[pl.ds(offset, count)], out_ref.at[pl.ds(start, count)], out_sem.at[i]
        )
        read.start()
        owners.append(owner)
        reads.append(read)
        writes.append(write)
        offset += count
    ready = meanwhile()
    hidden_in.wait()
    line = hid.shape[1] // (2 * OWNED // COLS)
    total, offset = jnp.zeros((line, COLS), jnp.float32), 0
    for owner, read, write, (_, _, _, first, count) in zip(owners, reads, writes, spots):
        rows = pl.ds(pl.multiple_of((owner & 1) * (OWNED // COLS * line), 16), OWNED // COLS * line)
        cut = hid[owner >> 1, rows, :].astype(jnp.float32)
        cut = [cut[c * line : (c + 1) * line] for c in range(first // COLS, (first + count) // COLS)]
        cut = jnp.concatenate(cut, axis=1).astype(jnp.bfloat16)
        read.wait()
        write.start()
        total = total + jnp.dot(
            cut, buf[offset : offset + count, :], preferred_element_type=jnp.float32
        )
        offset += count
    return total, writes, ready


def early_kernel(spots, follows, where_ref, moved_ref, *refs):
    if follows:
        before_ref, _, *refs = refs
    count = len(spots)
    out_ref, sum_ref, *work = refs[count:]
    total, writes, _ = place_pieces(spots, where_ref, moved_ref, refs[:count], out_ref, *work)
    sum_ref[...] = total + before_ref[...] if follows else total
    for write in writes:
        write.wait()


def late_kernel(spots, steps, rows, groups, where_ref, moved_ref, sum_ref, cos_ref, sin_ref, *refs):
    cached = [refs[4 * i : 4 * i + 4] for i in range(len(groups))]
    refs = refs[4 * len(groups) + 1 :]
    count = len(spots)
    out_ref, kv_ref, att_ref, turn, *work = refs[count:]
    heads = steps * rows * GROUPS

    def join(which):
        return jnp.concatenate(
            [
                group[which][s * n : (s + 1) * n].reshape(n * GROUPS, HD)
                for s in range(steps)
                for group, n in zip(cached, groups)
            ],
            axis=0,
        )

    def meanwhile():
        return join(1), join(2)[:, :1], join(3)[:, :1], sum_ref[...], cos_ref[...], sin_ref[...]

    total, writes, ready = place_pieces(
        spots, where_ref, moved_ref, refs[:count], out_ref, *work, meanwhile
    )
    acc, old_top, old_total, before, cosine, sine = ready
    total = total + before
    keys = total[:, :HD]
    keys = keys * cosine + pltpu.roll(keys, HD // 2, 1) * sine
    keys = keys.astype(jnp.bfloat16)
    values = total[:, HD:].astype(jnp.bfloat16)
    for s in range(steps):
        kv_ref[s, :, :HD] = keys[s * rows : (s + 1) * rows]
        kv_ref[s, :, HD:] = values[s * rows : (s + 1) * rows]
    scores = (
        lax.dot_general(
            cached[0][0][...].reshape(heads, HD),
            keys,
            (((1,), (1,)), ((), ())),
            preferred_element_type=jnp.float32,
        )
        * SCALE
    )
    line = lax.broadcasted_iota(jnp.int32, scores.shape, 0) // GROUPS
    column = lax.broadcasted_iota(jnp.int32, scores.shape, 1)
    seen = (line % rows == column % rows) & (column // rows <= line // rows)
    scores = jnp.where(seen, scores, -jnp.inf)
    top = jnp.maximum(old_top, jnp.max(scores, axis=-1, keepdims=True))
    fresh = jnp.exp(scores - top)
    fade = jnp.exp(old_top - top)
    denominator = old_total * fade + jnp.sum(fresh, axis=-1, keepdims=True)
    mixed = acc * (fade / denominator) + jnp.dot(
        (fresh / denominator).astype(jnp.bfloat16), values, preferred_element_type=jnp.float32
    )
    turn[...] = mixed
    for g in range(GROUPS):
        head = turn[pl.ds(g, steps * rows, stride=GROUPS), :].astype(jnp.bfloat16)
        for s in range(steps):
            att_ref[s, :, g * HD : (g + 1) * HD] = head[s * rows : (s + 1) * rows]
    for write in writes:
        write.wait()


def scratch(spots, moved):
    return [
        pltpu.VMEM((sum(s[4] for s in spots), COLS), jnp.bfloat16),
        pltpu.VMEM((TP, moved.shape[1] - ROWS, COLS), jnp.bfloat16),
        pltpu.SemaphoreType.DMA((len(spots) + 1,)),
        pltpu.SemaphoreType.DMA((len(spots),)),
    ]


def place_early(where, moved, before, pieces):
    spots = [p[1:] for p in pieces]
    lines = (moved.shape[1] - ROWS) * COLS // (2 * OWNED)
    return pl.pallas_call(
        lambda *refs: early_kernel(spots, bool(before), *refs),
        in_specs=[SMEM, ANY] + [VMEM, ANY][: len(before)] + [HBM] * len(pieces),
        out_specs=[ANY, VMEM],
        out_shape=[
            jax.ShapeDtypeStruct((REP * OWNED, COLS), jnp.bfloat16),
            jax.ShapeDtypeStruct((lines, COLS), jnp.float32),
        ],
        scratch_shapes=scratch(spots, moved),
        input_output_aliases={3: 0} if before else {},
        compiler_params=pltpu.CompilerParams(vmem_limit_bytes=PLACE_VMEM),
        cost_estimate=PLACE_COST,
    )(where, moved, *before, *[p[0] for p in pieces])


def place_late(where, moved, partial, cosine, sine, cached, placed, pieces, steps, rows, groups):
    spots = [p[1:] for p in pieces]
    small = 3 + 4 * len(groups)
    return pl.pallas_call(
        lambda *refs: late_kernel(spots, steps, rows, groups, *refs),
        in_specs=[SMEM, ANY] + [VMEM] * small + [ANY] + [HBM] * len(pieces),
        out_specs=[ANY, VMEM, VMEM],
        out_shape=[
            jax.ShapeDtypeStruct((REP * OWNED, COLS), jnp.bfloat16),
            jax.ShapeDtypeStruct((steps, rows, COLS), jnp.bfloat16),
            jax.ShapeDtypeStruct((steps, rows, GROUPS * HD), jnp.bfloat16),
        ],
        scratch_shapes=[
            pltpu.VMEM((steps * rows * GROUPS, HD), jnp.float32),
            *scratch(spots, moved),
        ],
        input_output_aliases={2 + small: 0},
        compiler_params=pltpu.CompilerParams(vmem_limit_bytes=PLACE_VMEM),
        cost_estimate=PLACE_COST,
    )(where, moved, partial, cosine, sine, *cached, placed, *[p[0] for p in pieces])


def exchange(pieces, *behind):
    held = lax.optimization_barrier(tuple(p[0] for p in pieces) + behind)
    pieces = [(v, *p[1:]) for v, p in zip(held, pieces)]
    other = [(send(p[0], CORE_SWAP), p[1], p[2], 1, p[4], p[5]) for p in pieces]
    return (pieces, other, *held[len(pieces) :])


def local(kv_master, hidden, queries, key_cache, value_cache, lengths):
    steps, rows, _ = hidden.shape
    where = lax.axis_index("rep").astype(jnp.int32).reshape(1)

    moved = lax.all_to_all(pack(kv_master, hidden), "tp", split_axis=0, concat_axis=0, tiled=True)
    owned = moved[:, :ROWS]
    cosine, sine = rotation_tables(lengths, steps)
    cached = attend_cache(queries, key_cache, value_cache, lengths, 0, rows)
    low, high = owned[: TP // 2].reshape(HALF, COLS), owned[TP // 2 :].reshape(HALF, COLS)
    owned, low, high, *cached = lax.optimization_barrier((owned, low, high, *cached))
    owned = owned.reshape(OWNED, COLS)

    up, down = z_shift(1), z_shift(-1)
    low_a, high_b = send(low, down), send(high, up)
    low_b, high_a = send(low, up), send(high, down)
    near_x = send(owned, X_SWAP)
    low_b, high_a, cosine, sine = lax.optimization_barrier((low_b, high_a, cosine, sine))
    below_x, above_x = send(near_x, up), send(near_x, down)
    far_low, far_high = send(low_b, up), send(high_a, down)
    far_low_x, far_high_x = send(far_low, X_SWAP), send(far_high, X_SWAP)

    near = [
        (owned, 0, 0, 0, 0, OWNED),
        (near_x, 0, 1, 0, 0, OWNED),
        (low_b, 3, 0, 0, 0, HALF),
        (high_a, 1, 0, 0, HALF, HALF),
        (low_a, 1, 0, 0, 0, HALF),
        (high_b, 3, 0, 0, HALF, HALF),
    ]
    far = [(far_low, 2, 0, 0, 0, HALF), (far_high, 2, 0, 0, HALF, HALF)]
    near, near_other = exchange(near)
    far, far_other = exchange(far)
    pieces = near + far + near_other + far_other
    placed, partial = place_early(where, moved, [], pieces)
    last = [
        (below_x, 3, 1, 0, 0, OWNED),
        (above_x, 1, 1, 0, 0, OWNED),
        (far_low_x, 2, 1, 0, 0, HALF),
        (far_high_x, 2, 1, 0, HALF, HALF),
    ]
    last, last_other, partial = exchange(last, partial)
    placed, partial = place_early(where, moved, [partial, placed], last)
    return tuple(
        place_late(
            where, moved, partial, cosine, sine, cached, placed, last_other, steps, rows, [rows]
        )
    )


def solution(mesh):
    return jax.shard_map(
        local,
        mesh=mesh,
        in_specs=(
            P(("rep", "tp"), None),
            P(None, "rep", "tp"),
            P(None, "rep", "tp"),
            P("rep", None, "tp"),
            P("rep", None, "tp"),
            P("rep"),
        ),
        out_specs=(P(None, "tp"), P(None, "rep", "tp"), P(None, "rep", "tp")),
        check_vma=False,
    )
```

```python
import math

import jax
import jax.numpy as jnp
from jax import lax
from jax.experimental import pallas as pl
from jax.experimental.pallas import tpu as pltpu
from jax.sharding import PartitionSpec as P

KVH = 8
HD = 128
QH = 128
GROUPS = QH // KVH
SCALE = HD ** (-0.5)

REP = 16
TP = 8
ROWS = 128
OWNED = TP * ROWS
HALF = OWNED // 2
COLS = 2 * HD
VMEM_BYTES = 60 * 2**20
PACK_STEPS = 4
CACHE_VMEM = 60 * 2**20
PLACE_VMEM = 48 * 2**20
PLACE_COST = pl.CostEstimate(flops=20000000000, bytes_accessed=1000, transcendentals=0)

rope_base = 500000.0

ANY = pl.BlockSpec(memory_space=pl.ANY)
HBM = pl.BlockSpec(memory_space=pltpu.HBM)
SMEM = pl.BlockSpec(memory_space=pltpu.SMEM)
VMEM = pl.BlockSpec(memory_space=pltpu.VMEM)


def z_shift(step):
    return [(r, ((((r >> 2) + step) % 4) << 2) | (r & 3)) for r in range(REP)]


X_SWAP = [(r, r ^ 2) for r in range(REP)]
CORE_SWAP = [(r, r ^ 1) for r in range(REP)]


def send(value, pairs):
    return lax.ppermute(value, "rep", pairs)


def scaled_frequencies(width):
    pair_index = jnp.arange(width // 2, dtype=jnp.float32)
    base_freq = rope_base ** (-2.0 * pair_index / width)
    wavelength = 2.0 * math.pi / base_freq
    smooth = (8192.0 / wavelength - 1.0) / 3.0
    blended = (1.0 - smooth) * base_freq / 8.0 + smooth * base_freq
    return jnp.where(
        wavelength < 2048.0, base_freq, jnp.where(wavelength > 8192.0, base_freq / 8.0, blended)
    )


def rotation_tables(lengths, steps):
    positions = lengths[None, :] + jnp.arange(steps, dtype=jnp.int32)[:, None]
    angles = positions.reshape(-1, 1).astype(jnp.float32) * scaled_frequencies(HD)
    cosine, sine = jnp.cos(angles), jnp.sin(angles)
    return (
        jnp.concatenate([cosine, cosine], axis=-1),
        jnp.concatenate([-sine, sine], axis=-1),
    )


def pack_kernel(kv_ref, hid_ref, out_ref):
    steps, _, width = hid_ref.shape
    flat = jnp.concatenate([hid_ref[s].astype(jnp.float32) for s in range(steps)], axis=0)
    cut = [flat[:, c : c + COLS] for c in range(0, width, COLS)]
    cut = jnp.concatenate(cut, axis=0).astype(jnp.bfloat16)
    for t in range(out_ref.shape[0]):
        out_ref[t, :ROWS] = kv_ref[:, t * COLS : (t + 1) * COLS].astype(jnp.bfloat16)
        out_ref[t, ROWS:] = cut


def pack(kv_master, hidden):
    shape = (TP, ROWS + hidden.size // COLS, COLS)
    return pl.pallas_call(
        pack_kernel,
        grid=(PACK_STEPS,),
        in_specs=[
            pl.BlockSpec((ROWS, TP * COLS // PACK_STEPS), lambda i: (0, i)),
            pl.BlockSpec(hidden.shape, lambda i: (0, 0, 0)),
        ],
        out_specs=pl.BlockSpec((TP // PACK_STEPS, *shape[1:]), lambda i: (i, 0, 0)),
        out_shape=jax.ShapeDtypeStruct(shape, jnp.bfloat16),
        compiler_params=pltpu.CompilerParams(vmem_limit_bytes=VMEM_BYTES),
    )(kv_master, hidden)


def cache_kernel(first, count, len_ref, q_ref, k_ref, v_ref, q_out, acc_out, m_out, l_out, q_scr, s_scr):
    i = pl.program_id(0)
    steps, rows = q_ref.shape[0], q_ref.shape[1]
    span = k_ref.shape[1]
    chunk = 2048

    @pl.when(i == 0)
    def _():
        flat = jnp.concatenate([q_ref[s].astype(jnp.float32) for s in range(steps)], axis=0)
        for g in range(GROUPS):
            q_scr[pl.ds(g, steps * rows, stride=GROUPS), :] = flat[:, g * HD : (g + 1) * HD]
        q_out[...] = q_scr[...].reshape(q_out.shape).astype(q_out.dtype)

    b = first + i
    base = [pl.multiple_of((s * rows + b) * GROUPS, GROUPS) for s in range(steps)]
    q = jnp.concatenate([q_scr[pl.ds(o, GROUPS), :] for o in base], axis=0).astype(jnp.bfloat16)
    length = len_ref[b]
    top = jnp.full((steps * GROUPS, 1), -jnp.inf, jnp.float32)
    for c in range(span // chunk):
        keys = k_ref[0, c * chunk : (c + 1) * chunk, :]
        scores = (
            lax.dot_general(q, keys, (((1,), (1,)), ((), ())), preferred_element_type=jnp.float32)
            * SCALE
        )
        place = c * chunk + lax.broadcasted_iota(jnp.int32, scores.shape, 1)
        scores = jnp.where(place < length, scores, -jnp.inf)
        s_scr[:, c * chunk : (c + 1) * chunk] = scores
        top = jnp.maximum(top, jnp.max(scores, axis=-1, keepdims=True))
    total = jnp.zeros((steps * GROUPS, 1), jnp.float32)
    acc = jnp.zeros((steps * GROUPS, HD), jnp.float32)
    for c in range(span // chunk):
        weights = jnp.exp(s_scr[:, c * chunk : (c + 1) * chunk] - top)
        total = total + jnp.sum(weights, axis=-1, keepdims=True)
        acc = acc + jnp.dot(
            weights.astype(jnp.bfloat16),
            v_ref[0, c * chunk : (c + 1) * chunk, :],
            preferred_element_type=jnp.float32,
        )
    for s in range(steps):
        part = slice(s * GROUPS, (s + 1) * GROUPS)
        place = s * count + i
        acc_out[place] = acc[part]
        m_out[place] = jnp.broadcast_to(top[part], (GROUPS, HD))
        l_out[place] = jnp.broadcast_to(total[part], (GROUPS, HD))


def attend_cache(queries, key_cache, value_cache, lengths, first, count):
    steps, rows, width = queries.shape
    span = key_cache.shape[1]
    part = jax.ShapeDtypeStruct((steps * count, GROUPS, HD), jnp.float32)
    return pl.pallas_call(
        lambda *refs: cache_kernel(first, count, *refs),
        grid=(count,),
        in_specs=[
            SMEM,
            pl.BlockSpec((steps, rows, width), lambda i: (0, 0, 0)),
            pl.BlockSpec((1, span, HD), lambda i: (first + i, 0, 0)),
            pl.BlockSpec((1, span, HD), lambda i: (first + i, 0, 0)),
        ],
        out_specs=[pl.BlockSpec((steps * rows, GROUPS, HD), lambda i: (0, 0, 0))]
        + [pl.BlockSpec(part.shape, lambda i: (0, 0, 0))] * 3,
        out_shape=[jax.ShapeDtypeStruct((steps * rows, GROUPS, HD), jnp.bfloat16)] + [part] * 3,
        scratch_shapes=[
            pltpu.VMEM((steps * rows * GROUPS, HD), jnp.float32),
            pltpu.VMEM((steps * GROUPS, span), jnp.float32),
        ],
        compiler_params=pltpu.CompilerParams(vmem_limit_bytes=CACHE_VMEM),
        cost_estimate=pl.CostEstimate(
            flops=4 * count * steps * GROUPS * span * HD,
            bytes_accessed=4 * count * span * HD,
            transcendentals=count * steps * GROUPS * span,
        ),
    )(lengths, queries, key_cache, value_cache)


def place_pieces(spots, where_ref, moved_ref, piece_refs, out_ref, buf, hid, in_sem, out_sem, meanwhile=tuple):
    rep = where_ref[0]
    hidden_in = pltpu.make_async_copy(moved_ref.at[:, pl.ds(ROWS, hid.shape[1])], hid, in_sem.at[len(spots)])
    hidden_in.start()
    owners, reads, writes, offset = [], [], [], 0
    for i, (dz, dx, dc, first, count) in enumerate(spots):
        owner = ((((rep >> 2) + dz) & 3) << 2) | ((rep & 3) ^ (2 * dx + dc))
        start = pl.multiple_of(owner * OWNED + first, ROWS)
        read = pltpu.make_async_copy(piece_refs[i], buf.at[pl.ds(offset, count)], in_sem.at[i])
        write = pltpu.make_async_copy(
            buf.at[pl.ds(offset, count)], out_ref.at[pl.ds(start, count)], out_sem.at[i]
        )
        read.start()
        owners.append(owner)
        reads.append(read)
        writes.append(write)
        offset += count
    ready = meanwhile()
    hidden_in.wait()
    line = hid.shape[1] // (2 * OWNED // COLS)
    total, offset = jnp.zeros((line, COLS), jnp.float32), 0
    for owner, read, write, (_, _, _, first, count) in zip(owners, reads, writes, spots):
        rows = pl.ds(pl.multiple_of((owner & 1) * (OWNED // COLS * line), 16), OWNED // COLS * line)
        cut = hid[owner >> 1, rows, :].astype(jnp.float32)
        cut = [cut[c * line : (c + 1) * line] for c in range(first // COLS, (first + count) // COLS)]
        cut = jnp.concatenate(cut, axis=1).astype(jnp.bfloat16)
        read.wait()
        write.start()
        total = total + jnp.dot(
            cut, buf[offset : offset + count, :], preferred_element_type=jnp.float32
        )
        offset += count
    return total, writes, ready


def early_kernel(spots, follows, where_ref, moved_ref, *refs):
    if follows:
        before_ref, _, *refs = refs
    count = len(spots)
    out_ref, sum_ref, *work = refs[count:]
    total, writes, _ = place_pieces(spots, where_ref, moved_ref, refs[:count], out_ref, *work)
    sum_ref[...] = total + before_ref[...] if follows else total
    for write in writes:
        write.wait()


def late_kernel(spots, steps, rows, groups, where_ref, moved_ref, sum_ref, cos_ref, sin_ref, *refs):
    cached = [refs[4 * i : 4 * i + 4] for i in range(len(groups))]
    refs = refs[4 * len(groups) + 1 :]
    count = len(spots)
    out_ref, kv_ref, att_ref, turn, *work = refs[count:]
    heads = steps * rows * GROUPS

    def join(which):
        return jnp.concatenate(
            [
                group[which][s * n : (s + 1) * n].reshape(n * GROUPS, HD)
                for s in range(steps)
                for group, n in zip(cached, groups)
            ],
            axis=0,
        )

    def meanwhile():
        return join(1), join(2)[:, :1], join(3)[:, :1], sum_ref[...], cos_ref[...], sin_ref[...]

    total, writes, ready = place_pieces(
        spots, where_ref, moved_ref, refs[:count], out_ref, *work, meanwhile
    )
    acc, old_top, old_total, before, cosine, sine = ready
    total = total + before
    keys = total[:, :HD]
    keys = keys * cosine + pltpu.roll(keys, HD // 2, 1) * sine
    keys = keys.astype(jnp.bfloat16)
    values = total[:, HD:].astype(jnp.bfloat16)
    for s in range(steps):
        kv_ref[s, :, :HD] = keys[s * rows : (s + 1) * rows]
        kv_ref[s, :, HD:] = values[s * rows : (s + 1) * rows]
    scores = (
        lax.dot_general(
            cached[0][0][...].reshape(heads, HD),
            keys,
            (((1,), (1,)), ((), ())),
            preferred_element_type=jnp.float32,
        )
        * SCALE
    )
    line = lax.broadcasted_iota(jnp.int32, scores.shape, 0) // GROUPS
    column = lax.broadcasted_iota(jnp.int32, scores.shape, 1)
    seen = (line % rows == column % rows) & (column // rows <= line // rows)
    scores = jnp.where(seen, scores, -jnp.inf)
    top = jnp.maximum(old_top, jnp.max(scores, axis=-1, keepdims=True))
    fresh = jnp.exp(scores - top)
    fade = jnp.exp(old_top - top)
    denominator = old_total * fade + jnp.sum(fresh, axis=-1, keepdims=True)
    mixed = acc * (fade / denominator) + jnp.dot(
        (fresh / denominator).astype(jnp.bfloat16), values, preferred_element_type=jnp.float32
    )
    turn[...] = mixed
    for g in range(GROUPS):
        head = turn[pl.ds(g, steps * rows, stride=GROUPS), :].astype(jnp.bfloat16)
        for s in range(steps):
            att_ref[s, :, g * HD : (g + 1) * HD] = head[s * rows : (s + 1) * rows]
    for write in writes:
        write.wait()


def scratch(spots, moved):
    return [
        pltpu.VMEM((sum(s[4] for s in spots), COLS), jnp.bfloat16),
        pltpu.VMEM((TP, moved.shape[1] - ROWS, COLS), jnp.bfloat16),
        pltpu.SemaphoreType.DMA((len(spots) + 1,)),
        pltpu.SemaphoreType.DMA((len(spots),)),
    ]


def place_early(where, moved, before, pieces):
    spots = [p[1:] for p in pieces]
    lines = (moved.shape[1] - ROWS) * COLS // (2 * OWNED)
    return pl.pallas_call(
        lambda *refs: early_kernel(spots, bool(before), *refs),
        in_specs=[SMEM, ANY] + [VMEM, ANY][: len(before)] + [HBM] * len(pieces),
        out_specs=[ANY, VMEM],
        out_shape=[
            jax.ShapeDtypeStruct((REP * OWNED, COLS), jnp.bfloat16),
            jax.ShapeDtypeStruct((lines, COLS), jnp.float32),
        ],
        scratch_shapes=scratch(spots, moved),
        input_output_aliases={3: 0} if before else {},
        compiler_params=pltpu.CompilerParams(vmem_limit_bytes=PLACE_VMEM),
        cost_estimate=PLACE_COST,
    )(where, moved, *before, *[p[0] for p in pieces])


def place_late(where, moved, partial, cosine, sine, cached, placed, pieces, steps, rows, groups):
    spots = [p[1:] for p in pieces]
    small = 3 + 4 * len(groups)
    return pl.pallas_call(
        lambda *refs: late_kernel(spots, steps, rows, groups, *refs),
        in_specs=[SMEM, ANY] + [VMEM] * small + [ANY] + [HBM] * len(pieces),
        out_specs=[ANY, VMEM, VMEM],
        out_shape=[
            jax.ShapeDtypeStruct((REP * OWNED, COLS), jnp.bfloat16),
            jax.ShapeDtypeStruct((steps, rows, COLS), jnp.bfloat16),
            jax.ShapeDtypeStruct((steps, rows, GROUPS * HD), jnp.bfloat16),
        ],
        scratch_shapes=[
            pltpu.VMEM((steps * rows * GROUPS, HD), jnp.float32),
            *scratch(spots, moved),
        ],
        input_output_aliases={2 + small: 0},
        compiler_params=pltpu.CompilerParams(vmem_limit_bytes=PLACE_VMEM),
        cost_estimate=PLACE_COST,
    )(where, moved, partial, cosine, sine, *cached, placed, *[p[0] for p in pieces])


def exchange(pieces, *behind):
    held = lax.optimization_barrier(tuple(p[0] for p in pieces) + behind)
    pieces = [(v, *p[1:]) for v, p in zip(held, pieces)]
    other = [(send(p[0], CORE_SWAP), p[1], p[2], 1, p[4], p[5]) for p in pieces]
    return (pieces, other, *held[len(pieces) :])


def local(kv_master, hidden, queries, key_cache, value_cache, lengths):
    steps, rows, _ = hidden.shape
    where = lax.axis_index("rep").astype(jnp.int32).reshape(1)

    moved = lax.all_to_all(pack(kv_master, hidden), "tp", split_axis=0, concat_axis=0, tiled=True)
    owned = moved[:, :ROWS]
    cosine, sine = rotation_tables(lengths, steps)
    cached = attend_cache(queries, key_cache, value_cache, lengths, 0, rows)
    low, high = owned[: TP // 2].reshape(HALF, COLS), owned[TP // 2 :].reshape(HALF, COLS)
    owned, low, high, *cached = lax.optimization_barrier((owned, low, high, *cached))
    owned = owned.reshape(OWNED, COLS)

    up, down = z_shift(1), z_shift(-1)
    low_a, high_b = send(low, down), send(high, up)
    low_b, high_a = send(low, up), send(high, down)
    near_x = send(owned, X_SWAP)
    low_b, high_a, cosine, sine = lax.optimization_barrier((low_b, high_a, cosine, sine))
    below_x, above_x = send(near_x, up), send(near_x, down)
    far_low, far_high = send(low_b, up), send(high_a, down)
    far_low_x, far_high_x = send(far_low, X_SWAP), send(far_high, X_SWAP)

    near = [
        (owned, 0, 0, 0, 0, OWNED),
        (near_x, 0, 1, 0, 0, OWNED),
        (low_b, 3, 0, 0, 0, HALF),
        (high_a, 1, 0, 0, HALF, HALF),
        (low_a, 1, 0, 0, 0, HALF),
        (high_b, 3, 0, 0, HALF, HALF),
    ]
    far = [(far_low, 2, 0, 0, 0, HALF), (far_high, 2, 0, 0, HALF, HALF)]
    near, near_other = exchange(near)
    far, far_other = exchange(far)
    pieces = near + far + near_other + far_other
    placed, partial = place_early(where, moved, [], pieces)
    last = [
        (below_x, 3, 1, 0, 0, OWNED),
        (above_x, 1, 1, 0, 0, OWNED),
        (far_low_x, 2, 1, 0, 0, HALF),
        (far_high_x, 2, 1, 0, HALF, HALF),
    ]
    last, last_other, partial = exchange(last, partial)
    placed, partial = place_early(where, moved, [partial, placed], last)
    return tuple(
        place_late(
            where, moved, partial, cosine, sine, cached, placed, last_other, steps, rows, [rows]
        )
    )


def solution(mesh):
    return jax.shard_map(
        local,
        mesh=mesh,
        in_specs=(
            P(("rep", "tp"), None),
            P(None, "rep", "tp"),
            P(None, "rep", "tp"),
            P("rep", None, "tp"),
            P("rep", None, "tp"),
            P("rep"),
        ),
        out_specs=(P(None, "tp"), P(None, "rep", "tp"), P(None, "rep", "tp")),
        check_vma=False,
    )
```
